32 devices in a mesh: groups: 2 (over x), wide: 8 (over z, y), narrow: 2 (over core).
Axes of the slice: x: 2, y: 2, z: 4, core: 2. Of those that a mesh axis runs over, the one named last changes fastest.
Arguments:
- tokens: bfloat16 [6656, 7168], P(('groups', 'wide', 'narrow')), parts along dimension 0, may hold values from -6 to 6
- norm_gain: float32 [7168], replicated, may hold values from 0.1 to 1.9
- routes: int32 [6656, 2], P(('groups', 'wide', 'narrow')), parts along dimension 0, may hold values from 0 to 127, all different within a row
- router_logits: float32 [6656, 2], P(('groups', 'wide', 'narrow')), parts along dimension 0, may hold values from -6 to 6
- gate_proj: bfloat16 [2, 7168, 4864], P('narrow', None, 'wide'), may hold values from -0.0625 to 0.0625
- up_proj: bfloat16 [2, 7168, 4864], P('narrow', None, 'wide'), may hold values from -0.0625 to 0.0625
- down_proj: bfloat16 [2, 4864, 7168], P('narrow', 'wide'), may hold values from -0.078125 to 0.078125
Outputs:
- layer_out: bfloat16 [6656, 7168], P(('groups', 'wide', 'narrow')), parts along dimension 0
The draws below stay inside these ranges and needn't reach their ends.
There are 2 independent parts, one for each index of `groups`. The reference program is written for one: setup_inputs(seed, part) draws one part's arguments, and reference() takes and returns one part's arrays. A program takes and returns all parts, laid end to end along the dimension named above; an argument that names none is the same for every part. Nothing has to cross between parts.
Inputs may be any that keep to these rules, and one draw needn't show every extreme that they name: `routes`: each token names two different experts.
All inputs are finite; a program needn't handle non-finite values.
Results may differ from the reference program's by a relative error of at most 0.006.
Values may be sent and summed in bfloat16 or wider, within the bound.
A program may use at most 128 MiB of HBM per device.

```python
import jax
import jax.numpy as jnp
from jax import lax

D = 7168
FF = 4864
EXPERTS_ALL = 128
TOK_DEV = 208
CAP = 8
FLIGHT = 2
TOKENS = 3328
N_WIDE = 8
N_NARROW = 2


def levels(rng, dims, cuts, least, top_value):
    def one(axis_at, shards_of):
        steps = jax.random.uniform(jax.random.fold_in(jax.random.fold_in(rng, 6), axis_at), (shards_of,), jnp.float32, least / len(cuts), top_value / len(cuts))
        return jnp.repeat(jnp.exp(steps), dims[axis_at] // shards_of).reshape((-1,) + (1,) * (len(dims) - axis_at - 1))

    loudness = one(*cuts[0])
    for cut in cuts[1:]:
        loudness = loudness * one(*cut)
    return loudness


def choose_distinct(key, rows, amount, top, lift):
    ranking = jax.random.permutation(jax.random.fold_in(key, 1), amount)
    boost = ranking
    for power in range(3):
        boost = boost * boost // amount
    boost = boost * lift // amount
    lots = jax.random.randint(jax.random.fold_in(key, 2), (rows, amount), 0, 4096) + boost
    sure = jax.random.permutation(jax.random.fold_in(key, 3), rows)[jnp.arange(amount) % rows]
    lots = jnp.where(jnp.arange(rows)[:, None] == sure[None, :], 1 << 14, lots)
    priority = lots * amount + jnp.arange(amount)
    return lax.top_k(priority.astype(jnp.int32), top)[1].astype(jnp.int32)


def bell_draw(rng, shape, deviation, bound, split=(), kind=jnp.bfloat16):
    loudness = levels(rng, shape, split, -0.22, 0.18) if split else 1.0
    values = jax.random.normal(rng, shape, jnp.float32) * deviation * loudness
    return jnp.minimum(jnp.maximum(values, -bound), bound).astype(kind)


def setup_inputs(seed: int = 0, part: int = 0) -> dict:
    keys = jax.random.split(jax.random.key(seed), 8)
    own_keys = jax.random.split(jax.random.fold_in(keys[7], part), 8)
    tokens = bell_draw(own_keys[0], (TOKENS, D), 1.0, 6.0, ((0, 16),))
    norm_gain = jnp.clip(1.0 + 0.18 * jax.random.normal(keys[1], (D,), jnp.float32), 0.1, 1.9)
    routes = choose_distinct(own_keys[2], TOKENS, EXPERTS_ALL, 2, 256)
    router_logits = bell_draw(own_keys[3], (TOKENS, 2), 1.5, 6.0, ((0, 16),), jnp.float32)
    gate_proj = bell_draw(keys[4], (FLIGHT, D, FF), D ** -0.5, 0.0625, ((0, 2), (2, 8)))
    up_proj = bell_draw(keys[5], (FLIGHT, D, FF), D ** -0.5, 0.0625, ((0, 2), (2, 8)))
    down_proj = bell_draw(keys[6], (FLIGHT, FF, D), FF ** -0.5, 0.078125, ((0, 2), (1, 8)))
    return dict(tokens=tokens, norm_gain=norm_gain, routes=routes, router_logits=router_logits, gate_proj=gate_proj, up_proj=up_proj, down_proj=down_proj)


def reference(tokens, norm_gain, routes, router_logits, gate_proj, up_proj, down_proj):
    block_count = N_WIDE * N_NARROW
    flight = N_NARROW
    wide_tok = tokens.astype(jnp.float32)
    scale = lax.rsqrt(lax.optimization_barrier(jnp.mean(wide_tok * wide_tok, axis=1, keepdims=True)) + 1e-05)
    normed = (wide_tok * scale * norm_gain.astype(jnp.float32)).astype(jnp.bfloat16)
    probs = jax.nn.softmax(router_logits.astype(jnp.float32), axis=1)
    expert_ids = jnp.arange(flight, dtype=jnp.int32)
    hits = routes[:, :, None] == expert_ids[None, None, :]
    matched = lax.optimization_barrier(jnp.sum(hits.astype(jnp.int32), axis=1))
    blocked = matched.reshape(block_count, TOK_DEV, flight)
    slot_rank = (jnp.cumsum(blocked, axis=1) - 1).reshape(TOKENS, flight)
    is_kept = (matched > 0) & (slot_rank < CAP)
    slot_ids = jnp.arange(CAP, dtype=jnp.int32)
    select = (is_kept[:, :, None] & (slot_rank[:, :, None] == slot_ids[None, None, :])).astype(jnp.float32)
    weights = lax.optimization_barrier(jnp.sum(hits.astype(jnp.float32) * probs[:, :, None], axis=1)) * is_kept.astype(jnp.float32)
    select_blocks = select.reshape(block_count, TOK_DEV, flight, CAP)
    normed_blocks = normed.astype(jnp.float32).reshape(block_count, TOK_DEV, D)
    buffer = jnp.einsum('jtfc,jtd->fjcd', select_blocks, normed_blocks)
    buffer = buffer.reshape(flight, block_count * CAP, D).astype(jnp.bfloat16)
    width = FF // N_WIDE
    results = []
    for expert in range(flight):
        gate_act = jnp.dot(buffer[expert], gate_proj[expert], preferred_element_type=jnp.float32)
        up_act = jnp.dot(buffer[expert], up_proj[expert], preferred_element_type=jnp.float32)
        hidden = (jax.nn.silu(gate_act) * up_act).astype(jnp.bfloat16)
        down_one = down_proj[expert]

        def add_block(index, total):
            start = (index * width).astype(jnp.int32)
            columns = lax.dynamic_slice_in_dim(hidden, start, width, 1)
            rows = lax.dynamic_slice_in_dim(down_one, start, width, 0)
            part = jnp.dot(columns, rows, preferred_element_type=jnp.float32).astype(jnp.bfloat16)
            part = lax.optimization_barrier(part)
            return total + part.astype(jnp.float32)
        summed = lax.fori_loop(0, N_WIDE, add_block, jnp.zeros((block_count * CAP, D), jnp.float32))
        results.append(summed.astype(jnp.bfloat16))
    expert_out = jnp.stack(results).astype(jnp.float32).reshape(flight, block_count, CAP, D)
    coefs = (select * weights[:, :, None]).reshape(block_count, TOK_DEV, flight, CAP)
    combined = jnp.einsum('jtfc,fjcd->jtd', coefs, expert_out, precision=lax.Precision.HIGHEST)
    return (wide_tok + combined.reshape(TOKENS, D)).astype(jnp.bfloat16)
```

```python
import functools

import jax
import jax.numpy as jnp
from jax import lax
from jax.experimental import pallas as pl
from jax.experimental.pallas import tpu as pltpu
from jax.sharding import PartitionSpec as P

CAP = 8
N_CHUNKS = 4
MESH = pl.DeviceIdType.MESH
F32 = jnp.float32
BF16 = jnp.bfloat16


def normalize(tokens, norm_gain):
    wide_tok = tokens.astype(jnp.float32)
    scale = lax.rsqrt(jnp.mean(wide_tok * wide_tok, axis=1, keepdims=True) + 1e-05)
    return (wide_tok * scale * norm_gain).astype(jnp.bfloat16)


def slot_tables(routes, router_logits, flight, capacity):
    probs = jax.nn.softmax(router_logits, axis=1)
    expert_ids = lax.broadcasted_iota(jnp.int32, (1, 1, flight), 2)
    hits = routes[:, :, None] == expert_ids
    matched = jnp.sum(hits.astype(jnp.int32), axis=1)
    slot_rank = jnp.cumsum(matched, axis=0) - 1
    is_kept = (matched > 0) & (slot_rank < capacity)
    slot_ids = lax.broadcasted_iota(jnp.int32, (1, 1, capacity), 2)
    select = is_kept[:, :, None] & (slot_rank[:, :, None] == slot_ids)
    weights = jnp.sum(hits.astype(jnp.float32) * probs[:, :, None], axis=1) * is_kept.astype(
        jnp.float32
    )
    return (select, weights)


def expert_hidden(rows, gate_local, up_local):
    gate_act = jnp.dot(rows, gate_local, preferred_element_type=jnp.float32)
    up_act = jnp.dot(rows, up_local, preferred_element_type=jnp.float32)
    return (jax.nn.silu(gate_act) * up_act).astype(jnp.bfloat16)


def shards(tokens, norm_gain, routes, router_logits, gate_proj, up_proj, down_proj):
    flight = lax.axis_size("narrow")
    normed = normalize(tokens, norm_gain)
    select, weights = slot_tables(routes, router_logits, flight, CAP)
    buffer = jnp.einsum(
        "tfc,td->fcd", select.astype(jnp.bfloat16), normed, preferred_element_type=jnp.float32
    ).astype(jnp.bfloat16)
    gate_local = gate_proj[0]
    up_local = up_proj[0]
    owned = lax.all_to_all(buffer, "narrow", split_axis=0, concat_axis=1, tiled=True)
    hidden_all = expert_hidden(
        lax.all_gather(owned, "wide", axis=1, tiled=True)[0], gate_local, up_local
    )
    down_local = down_proj[0]
    summed = lax.psum_scatter(
        jnp.dot(hidden_all, down_local, preferred_element_type=jnp.float32).astype(jnp.bfloat16),
        "wide",
        scatter_dimension=0,
        tiled=True,
    )
    expert_out = summed.reshape(flight, CAP, summed.shape[1])
    returned = lax.all_to_all(expert_out, "narrow", split_axis=0, concat_axis=0, tiled=True)
    coefs = select.astype(jnp.float32) * weights[:, :, None]
    combined = jnp.einsum(
        "tfc,fcd->td", coefs, returned.astype(jnp.float32), precision=lax.Precision.HIGHEST
    )
    return (tokens.astype(jnp.float32) + combined).astype(jnp.bfloat16)


def picks(routes, narrow):
    count = routes.shape[1]
    row = lax.broadcasted_iota(jnp.int32, (2 * CAP, count), 0)
    own = row < CAP
    expert = jnp.where(own, narrow, 1 - narrow)
    slot = jnp.where(own, row, row - CAP)
    first = routes[0:1, :] == expert
    second = routes[1:2, :] == expert
    hit = first | second
    earlier = lax.broadcasted_iota(jnp.int32, (count, count), 0) < lax.broadcasted_iota(
        jnp.int32, (count, count), 1
    )
    rank = jnp.dot(
        jnp.where(hit, 1.0, 0.0).astype(BF16),
        jnp.where(earlier, 1.0, 0.0).astype(BF16),
        preferred_element_type=F32,
    )
    return first, second, hit & (rank == slot.astype(F32))


def fold(rows):
    half = rows.shape[1] // 2
    return jnp.concatenate([rows[:, :half], rows[:, half:]], axis=0).astype(BF16)


def unfold(packed):
    wide = packed.astype(F32)
    return jnp.concatenate([wide[:CAP], wide[CAP:]], axis=1)


def experts(
    n_z, n_c, tokens_hbm, gain, routes, gate_hbm, up_hbm, down_hbm, out,
    tok, gate, up, down, raw, give, got, gathered, gate_acc, up_acc, hidden,
    own_part, y_send, y_recv, z_send, z_recv, back_send, back_recv,
    tok_sem, w_sem, d_sem, x_sem, gz_send, gz_recv, gy_send, gy_recv,
    ry_sem, rz_send, rz_recv, b_sem,
):
    wide, narrow = lax.axis_index("wide"), lax.axis_index("narrow")
    z, y = lax.div(wide, 2), lax.rem(wide, 2)
    width = tok.shape[2]
    rows = 2 * CAP
    y_peer = {"wide": 2 * z + 1 - y}
    sibling = {"narrow": 1 - narrow}
    z_at = [lax.rem(z + step, n_z) for step in range(n_z)]
    z_from = [lax.rem(z + n_z - step, n_z) for step in range(n_z)]

    def z_peer(step):
        return {"wide": 2 * z_at[step] + y}

    def remote(source, target, send, recv, device):
        return pltpu.make_async_remote_copy(
            src_ref=source, dst_ref=target, send_sem=send, recv_sem=recv,
            device_id=device, device_id_type=MESH,
        )

    def columns(k):
        return pl.ds(pl.multiple_of(k * width, 128), width)

    def token_copy(k):
        return pltpu.make_async_copy(tokens_hbm.at[:, columns(k)], tok.at[k], tok_sem.at[k])

    def weight_copies(k):
        return (
            pltpu.make_async_copy(gate_hbm.at[0, :, columns(k)], gate.at[k], w_sem.at[0, k]),
            pltpu.make_async_copy(up_hbm.at[0, :, columns(k)], up.at[k], w_sem.at[1, k]),
        )

    def down_copy(k):
        return pltpu.make_async_copy(down_hbm.at[0, :, columns(k)], down.at[k], d_sem.at[k])

    def exchange(k):
        return remote(give.at[k], got.at[k], x_sem.at[0, k], x_sem.at[1, k], sibling)

    def along_z(k, step):
        return remote(
            gathered.at[k, z], gathered.at[k, z], gz_send.at[step, k], gz_recv.at[z, k], z_peer(step)
        )

    def from_z(k, step):
        at = z_from[step]
        return remote(
            gathered.at[k, at], gathered.at[k, at], gz_send.at[step, k], gz_recv.at[at, k], z_peer(step)
        )

    def along_y(k, at):
        return remote(
            gathered.at[k, at], gathered.at[k, n_z + at], gy_send.at[at, k], gy_recv.at[at, k], y_peer
        )

    def sum_y(k):
        return remote(y_send.at[k], y_recv.at[k], ry_sem.at[0, k], ry_sem.at[1, k], y_peer)

    def sum_z(k, step):
        return remote(
            z_send.at[k, z_at[step]], z_recv.at[k, step], rz_send.at[step, k], rz_recv.at[step, k],
            z_peer(step),
        )

    def hand_back(k):
        return remote(back_send.at[k], back_recv.at[k], b_sem.at[0, k], b_sem.at[1, k], sibling)

    for k in range(n_c):
        token_copy(k).start()
    barrier = pltpu.get_barrier_semaphore()
    for peer in [sibling, y_peer] + [z_peer(step) for step in range(1, n_z)]:
        pl.semaphore_signal(barrier, inc=1, device_id=peer, device_id_type=MESH)
    pl.semaphore_wait(barrier, n_z + 1)

    _, _, chosen = picks(routes[...], narrow)
    chosen = jnp.where(chosen, 1.0, 0.0).astype(BF16)
    squares = jnp.zeros((rows, 1), F32)
    for k in range(n_c):
        token_copy(k).wait()
        picked = jnp.dot(chosen, tok[k], preferred_element_type=F32)
        raw[k] = picked
        squares = squares + jnp.sum(picked * picked, axis=1, keepdims=True)
    for k in range(n_c):
        for copy in weight_copies(k):
            copy.start()
    for k in range(n_c):
        down_copy(k).start()
    scale = lax.rsqrt(squares / (n_c * width) + 1e-05)
    for k in range(n_c):
        normed = raw[k] * scale * gain[0:1, k * width : (k + 1) * width]
        raw[k] = normed
        give[k] = fold(normed[CAP:])
        exchange(k).start()
    for k in range(n_c):
        exchange(k).wait_recv()
        gathered[k, z] = jnp.concatenate([raw[k, :CAP], unfold(got[k])], axis=0).astype(BF16)
        along_y(k, z).start()
        for step in range(1, n_z):
            along_z(k, step).start()
    gate_acc[...] = jnp.zeros_like(gate_acc)
    up_acc[...] = jnp.zeros_like(up_acc)

    def pass_on(k):
        for step in range(1, n_z):
            from_z(k, step).wait_recv()
            along_y(k, z_from[step]).start()

    pass_on(0)

    def take(k, carry):
        @pl.when(k + 1 < n_c)
        def _():
            pass_on(k + 1)

        for step in range(n_z):
            along_y(k, z_from[step]).wait_recv()
        for copy in weight_copies(k):
            copy.wait()
        block = gathered[k].reshape(2 * n_z * rows, width)
        gate_acc[...] += lax.dot_general(
            block, gate[k], (((1,), (1,)), ((), ())), preferred_element_type=F32
        )
        up_acc[...] += lax.dot_general(
            block, up[k], (((1,), (1,)), ((), ())), preferred_element_type=F32
        )
        return carry

    lax.fori_loop(0, n_c, take, 0)
    gated = gate_acc[...]
    hidden[...] = (gated / (1.0 + jnp.exp(-gated)) * up_acc[...]).astype(BF16)

    def part(k, carry):
        down_copy(k).wait()
        product = jnp.dot(hidden[...], down[k], preferred_element_type=F32)
        half = n_z * rows
        y_send[k] = product[half:].astype(BF16).reshape(n_z, rows, width)
        sum_y(k).start()
        own_part[k] = product[:half].reshape(n_z, rows, width)
        return carry

    lax.fori_loop(0, n_c, part, 0)

    def pair_up(k):
        sum_y(k).wait_recv()
        both = own_part[k] + y_recv[k].astype(F32)
        own_part[k] = both
        z_send[k] = both.astype(BF16)
        for step in range(1, n_z):
            sum_z(k, step).start()

    def finish(k):
        total = own_part[k, z]
        for step in range(1, n_z):
            sum_z(k, step).wait_recv()
            total = total + z_recv[k, step].astype(F32)
        raw[k] = total
        back_send[k] = fold(total[CAP:])
        hand_back(k).start()

    def collect(k):
        hand_back(k).wait_recv()
        out[:, k * width : (k + 1) * width] = jnp.concatenate(
            [raw[k, :CAP], unfold(back_recv[k])], axis=0
        ).astype(BF16)

    pair_up(0)
    for k in range(n_c):
        if k + 1 < n_c:
            pair_up(k + 1)
        finish(k)
        if k >= 1:
            collect(k - 1)
    collect(n_c - 1)

    for k in range(n_c):
        exchange(k).wait_send()
        for step in range(n_z):
            along_y(k, z_from[step]).wait_send()
        for step in range(1, n_z):
            along_z(k, step).wait_send()
            sum_z(k, step).wait_send()
        sum_y(k).wait_send()
        hand_back(k).wait_send()


def combine(narrow, routes, logits, tokens, expert_out, out, coefs):
    @pl.when(pl.program_id(0) == 0)
    def _():
        first, second, chosen = picks(routes[...], narrow[0])
        values = logits[...]
        powers = jnp.exp(values - jnp.max(values, axis=0, keepdims=True))
        probs = powers / jnp.sum(powers, axis=0, keepdims=True)
        weight = jnp.where(first, probs[0:1, :], 0.0) + jnp.where(second, probs[1:2, :], 0.0)
        rest = jnp.where(chosen, weight, 0.0)
        for piece in range(3):
            rounded = rest.astype(BF16)
            coefs[piece * 2 * CAP : (piece + 1) * 2 * CAP, :] = rounded
            rest = rest - rounded.astype(F32)

    rows = expert_out[...]
    added = lax.dot_general(
        coefs[...],
        jnp.concatenate([rows, rows, rows], axis=0),
        (((0,), (0,)), ((), ())),
        preferred_element_type=F32,
    )
    out[...] = (tokens[...].astype(F32) + added).astype(BF16)


def fused(n_z, tokens, norm_gain, routes, router_logits, gate_proj, up_proj, down_proj):
    n_c = N_CHUNKS
    count, depth = tokens.shape
    width = depth // n_c
    units = gate_proj.shape[2]
    rows = 2 * CAP
    everyone = 2 * n_z * rows
    vmem, hbm = pl.BlockSpec(memory_space=pltpu.VMEM), pl.BlockSpec(memory_space=pl.ANY)
    dma = pltpu.SemaphoreType.DMA
    routes_t, logits_t = routes.T, router_logits.T
    expert_out = pl.pallas_call(
        functools.partial(experts, n_z, n_c),
        out_shape=jax.ShapeDtypeStruct((rows, depth), BF16),
        in_specs=[hbm, vmem, vmem, hbm, hbm, hbm],
        out_specs=vmem,
        scratch_shapes=[
            pltpu.VMEM((n_c, count, width), BF16),
            pltpu.VMEM((n_c, units, width), BF16),
            pltpu.VMEM((n_c, units, width), BF16),
            pltpu.VMEM((n_c, units, width), BF16),
            pltpu.VMEM((n_c, rows, width), F32),
            pltpu.VMEM((n_c, rows, width // 2), BF16),
            pltpu.VMEM((n_c, rows, width // 2), BF16),
            pltpu.VMEM((n_c, 2 * n_z, rows, width), BF16),
            pltpu.VMEM((everyone, units), F32),
            pltpu.VMEM((everyone, units), F32),
            pltpu.VMEM((everyone, units), BF16),
            pltpu.VMEM((n_c, n_z, rows, width), F32),
            pltpu.VMEM((n_c, n_z, rows, width), BF16),
            pltpu.VMEM((n_c, n_z, rows, width), BF16),
            pltpu.VMEM((n_c, n_z, rows, width), BF16),
            pltpu.VMEM((n_c, n_z, rows, width), BF16),
            pltpu.VMEM((n_c, rows, width // 2), BF16),
            pltpu.VMEM((n_c, rows, width // 2), BF16),
            dma((n_c,)),
            dma((2, n_c)),
            dma((n_c,)),
            dma((2, n_c)),
            dma((n_z, n_c)),
            dma((n_z, n_c)),
            dma((n_z, n_c)),
            dma((n_z, n_c)),
            dma((2, n_c)),
            dma((n_z, n_c)),
            dma((n_z, n_c)),
            dma((2, n_c)),
        ],
        compiler_params=pltpu.CompilerParams(
            collective_id=0, has_side_effects=True, vmem_limit_bytes=58 * 1024 * 1024
        ),
    )(
        tokens, norm_gain.reshape(1, depth), routes_t,
        jnp.swapaxes(gate_proj, 1, 2), jnp.swapaxes(up_proj, 1, 2), down_proj,
    )
    tile = depth // 7
    narrow = lax.axis_index("narrow").astype(jnp.int32).reshape(1)
    return pl.pallas_call(
        combine,
        grid=(7,),
        out_shape=jax.ShapeDtypeStruct(tokens.shape, BF16),
        in_specs=[
            pl.BlockSpec(memory_space=pltpu.SMEM),
            vmem,
            vmem,
            pl.BlockSpec((count, tile), lambda i: (0, i)),
            pl.BlockSpec((rows, tile), lambda i: (0, i)),
        ],
        out_specs=pl.BlockSpec((count, tile), lambda i: (0, i)),
        scratch_shapes=[pltpu.VMEM((3 * rows, count), BF16)],
    )(narrow, routes_t, logits_t, tokens, expert_out)


def solution(mesh):
    placed = (
        P(("groups", "wide", "narrow"), None),
        P(),
        P(("groups", "wide", "narrow"), None),
        P(("groups", "wide", "narrow"), None),
        P("narrow", None, "wide"),
        P("narrow", None, "wide"),
        P("narrow", "wide", None),
    )
    fits = mesh.shape["wide"] == 8 and mesh.shape["narrow"] == 2
    return jax.shard_map(
        functools.partial(fused, mesh.shape["wide"] // 2) if fits else shards,
        mesh=mesh,
        in_specs=placed,
        out_specs=P(("groups", "wide", "narrow"), None),
        check_vma=False,
    )
```

```python
import functools

import jax
import jax.numpy as jnp
from jax import lax
from jax.experimental import pallas as pl
from jax.experimental.pallas import tpu as pltpu
from jax.sharding import PartitionSpec as P

CAP = 8
N_CHUNKS = 4
SUM_WIDTHS = (1792, 1792, 1792, 1792)
MESH = pl.DeviceIdType.MESH
F32 = jnp.float32
BF16 = jnp.bfloat16


def normalize(tokens, norm_gain):
    wide_tok = tokens.astype(jnp.float32)
    scale = lax.rsqrt(jnp.mean(wide_tok * wide_tok, axis=1, keepdims=True) + 1e-05)
    return (wide_tok * scale * norm_gain).astype(jnp.bfloat16)


def slot_tables(routes, router_logits, flight, capacity):
    probs = jax.nn.softmax(router_logits, axis=1)
    expert_ids = lax.broadcasted_iota(jnp.int32, (1, 1, flight), 2)
    hits = routes[:, :, None] == expert_ids
    matched = jnp.sum(hits.astype(jnp.int32), axis=1)
    slot_rank = jnp.cumsum(matched, axis=0) - 1
    is_kept = (matched > 0) & (slot_rank < capacity)
    slot_ids = lax.broadcasted_iota(jnp.int32, (1, 1, capacity), 2)
    select = is_kept[:, :, None] & (slot_rank[:, :, None] == slot_ids)
    weights = jnp.sum(hits.astype(jnp.float32) * probs[:, :, None], axis=1) * is_kept.astype(
        jnp.float32
    )
    return (select, weights)


def expert_hidden(rows, gate_local, up_local):
    gate_act = jnp.dot(rows, gate_local, preferred_element_type=jnp.float32)
    up_act = jnp.dot(rows, up_local, preferred_element_type=jnp.float32)
    return (jax.nn.silu(gate_act) * up_act).astype(jnp.bfloat16)


def shards(tokens, norm_gain, routes, router_logits, gate_proj, up_proj, down_proj):
    flight = lax.axis_size("narrow")
    normed = normalize(tokens, norm_gain)
    select, weights = slot_tables(routes, router_logits, flight, CAP)
    buffer = jnp.einsum(
        "tfc,td->fcd", select.astype(jnp.bfloat16), normed, preferred_element_type=jnp.float32
    ).astype(jnp.bfloat16)
    gate_local = gate_proj[0]
    up_local = up_proj[0]
    owned = lax.all_to_all(buffer, "narrow", split_axis=0, concat_axis=1, tiled=True)
    hidden_all = expert_hidden(
        lax.all_gather(owned, "wide", axis=1, tiled=True)[0], gate_local, up_local
    )
    down_local = down_proj[0]
    summed = lax.psum_scatter(
        jnp.dot(hidden_all, down_local, preferred_element_type=jnp.float32).astype(jnp.bfloat16),
        "wide",
        scatter_dimension=0,
        tiled=True,
    )
    expert_out = summed.reshape(flight, CAP, summed.shape[1])
    returned = lax.all_to_all(expert_out, "narrow", split_axis=0, concat_axis=0, tiled=True)
    coefs = select.astype(jnp.float32) * weights[:, :, None]
    combined = jnp.einsum(
        "tfc,fcd->td", coefs, returned.astype(jnp.float32), precision=lax.Precision.HIGHEST
    )
    return (tokens.astype(jnp.float32) + combined).astype(jnp.bfloat16)


def picks(routes, narrow):
    count = routes.shape[1]
    row = lax.broadcasted_iota(jnp.int32, (2 * CAP, count), 0)
    own = row < CAP
    expert = jnp.where(own, narrow, 1 - narrow)
    slot = jnp.where(own, row, row - CAP)
    first = routes[0:1, :] == expert
    second = routes[1:2, :] == expert
    hit = first | second
    earlier = lax.broadcasted_iota(jnp.int32, (count, count), 0) < lax.broadcasted_iota(
        jnp.int32, (count, count), 1
    )
    rank = jnp.dot(
        jnp.where(hit, 1.0, 0.0).astype(BF16),
        jnp.where(earlier, 1.0, 0.0).astype(BF16),
        preferred_element_type=F32,
    )
    return first, second, hit & (rank == slot.astype(F32))


def fold(rows):
    half = rows.shape[1] // 2
    return jnp.concatenate([rows[:, :half], rows[:, half:]], axis=0).astype(BF16)


def unfold(packed):
    wide = packed.astype(F32)
    return jnp.concatenate([wide[:CAP], wide[CAP:]], axis=1)


def experts(
    n_z, n_c, n_s, tokens_hbm, gain, routes, logits, gate_hbm, up_hbm, down_hbm, out, coefs,
    tok, gate, up, down, raw, give, got, gathered, gate_acc, up_acc, hidden,
    own_part, y_send, y_recv, z_send, z_recv, back_send, back_recv,
    tok_sem, w_sem, d_sem, x_sem, gz_send, gz_recv, gy_send, gy_recv,
    ry_sem, rz_send, rz_recv, b_sem,
):
    wide, narrow = lax.axis_index("wide"), lax.axis_index("narrow")
    z, y = lax.div(wide, 2), lax.rem(wide, 2)
    width = tok.shape[2]
    rows = 2 * CAP
    y_peer = {"wide": 2 * z + 1 - y}
    sibling = {"narrow": 1 - narrow}
    z_at = [lax.rem(z + step, n_z) for step in range(n_z)]
    z_from = [lax.rem(z + n_z - step, n_z) for step in range(n_z)]

    def z_peer(step):
        return {"wide": 2 * z_at[step] + y}

    def remote(source, target, send, recv, device):
        return pltpu.make_async_remote_copy(
            src_ref=source, dst_ref=target, send_sem=send, recv_sem=recv,
            device_id=device, device_id_type=MESH,
        )

    def columns(k):
        return pl.ds(pl.multiple_of(k * width, 128), width)

    def token_copy(k):
        return pltpu.make_async_copy(tokens_hbm.at[:, columns(k)], tok.at[k], tok_sem.at[k])

    def weight_copies(k):
        return (
            pltpu.make_async_copy(gate_hbm.at[0, :, columns(k)], gate.at[k], w_sem.at[0, k]),
            pltpu.make_async_copy(up_hbm.at[0, :, columns(k)], up.at[k], w_sem.at[1, k]),
        )

    starts = [sum(SUM_WIDTHS[:j]) for j in range(n_s)]
    spans = [pl.ds(starts[j], SUM_WIDTHS[j]) for j in range(n_s)]

    def down_copy(j):
        return pltpu.make_async_copy(down_hbm.at[0, :, spans[j]], down.at[:, spans[j]], d_sem.at[j])

    def exchange(k):
        return remote(give.at[k], got.at[k], x_sem.at[0, k], x_sem.at[1, k], sibling)

    def along_z(k, step):
        return remote(
            gathered.at[k, z], gathered.at[k, z], gz_send.at[step, k], gz_recv.at[z, k], z_peer(step)
        )

    def from_z(k, step):
        at = z_from[step]
        return remote(
            gathered.at[k, at], gathered.at[k, at], gz_send.at[step, k], gz_recv.at[at, k], z_peer(step)
        )

    def along_y(k, at):
        return remote(
            gathered.at[k, at], gathered.at[k, n_z + at], gy_send.at[at, k], gy_recv.at[at, k], y_peer
        )

    def sum_y(j):
        return remote(
            y_send[j], y_recv[j], ry_sem.at[0, j], ry_sem.at[1, j],
            y_peer,
        )

    def sum_z(j, step):
        return remote(
            z_send[j].at[z_at[step]], z_recv[j].at[step], rz_send.at[step, j],
            rz_recv.at[step, j], z_peer(step),
        )

    def hand_back(j):
        return remote(
            back_send[j], back_recv[j], b_sem.at[0, j], b_sem.at[1, j],
            sibling,
        )

    for k in range(n_c):
        token_copy(k).start()
    barrier = pltpu.get_barrier_semaphore()
    for peer in [sibling, y_peer] + [z_peer(step) for step in range(1, n_z)]:
        pl.semaphore_signal(barrier, inc=1, device_id=peer, device_id_type=MESH)

    first, second, kept = picks(routes[...], narrow)
    chosen = jnp.where(kept, 1.0, 0.0).astype(BF16)
    squares = jnp.zeros((rows, 1), F32)
    for k in range(n_c):
        token_copy(k).wait()
        picked = jnp.dot(chosen, tok[k], preferred_element_type=F32)
        raw[:, k * width : (k + 1) * width] = picked
        squares = squares + jnp.sum(picked * picked, axis=1, keepdims=True)
    for k in range(n_c):
        for copy in weight_copies(k):
            copy.start()
    for j in range(n_s):
        down_copy(j).start()
    pl.semaphore_wait(barrier, n_z + 1)
    scale = lax.rsqrt(squares / (n_c * width) + 1e-05)
    for k in range(n_c):
        normed = raw[:, k * width : (k + 1) * width] * scale * gain[0:1, k * width : (k + 1) * width]
        raw[:, k * width : (k + 1) * width] = normed
        give[k] = fold(normed[CAP:])
        exchange(k).start()
    for k in range(n_c):
        exchange(k).wait_recv()
        gathered[k, z] = jnp.concatenate(
            [raw[:CAP, k * width : (k + 1) * width], unfold(got[k])], axis=0
        ).astype(BF16)
        along_y(k, z).start()
        for step in range(1, n_z):
            along_z(k, step).start()
    values = logits[...]
    powers = jnp.exp(values - jnp.max(values, axis=0, keepdims=True))
    probs = powers / jnp.sum(powers, axis=0, keepdims=True)
    weight = jnp.where(first, probs[0:1, :], 0.0) + jnp.where(second, probs[1:2, :], 0.0)
    rest = jnp.where(kept, weight, 0.0)
    pieces = []
    for _ in range(3):
        rounded = rest.astype(BF16).astype(F32)
        pieces.append(rounded)
        rest = rest - rounded
    coefs[...] = jnp.concatenate(pieces, axis=0).T.astype(BF16)
    gate_acc[...] = jnp.zeros_like(gate_acc)
    up_acc[...] = jnp.zeros_like(up_acc)

    def pass_on(k):
        for step in range(1, n_z):
            from_z(k, step).wait_recv()
            along_y(k, z_from[step]).start()

    pass_on(0)

    def take(k, carry):
        @pl.when(k + 1 < n_c)
        def _():
            pass_on(k + 1)

        for step in range(n_z):
            along_y(k, z_from[step]).wait_recv()
        for copy in weight_copies(k):
            copy.wait()
        block = gathered[k].reshape(2 * n_z * rows, width)
        gate_acc[...] += lax.dot_general(
            block, gate[k], (((1,), (1,)), ((), ())), preferred_element_type=F32
        )
        up_acc[...] += lax.dot_general(
            block, up[k], (((1,), (1,)), ((), ())), preferred_element_type=F32
        )
        return carry

    lax.fori_loop(0, n_c, take, 0)
    gated = gate_acc[...]
    hidden[...] = (gated / (1.0 + jnp.exp(-gated)) * up_acc[...]).astype(BF16)

    half = n_z * rows
    for j in range(n_s):
        down_copy(j).wait()
        product = jnp.dot(hidden[...], down[:, spans[j]], preferred_element_type=F32)
        y_send[j][...] = product[half:].astype(BF16).reshape(n_z, rows, SUM_WIDTHS[j])
        sum_y(j).start()
        own_part[j][...] = product[:half].reshape(n_z, rows, SUM_WIDTHS[j])

    def pair_up(j):
        sum_y(j).wait_recv()
        both = own_part[j][...] + y_recv[j][...].astype(F32)
        own_part[j][...] = both
        z_send[j][...] = both.astype(BF16)
        for step in range(1, n_z):
            sum_z(j, step).start()

    def finish(j):
        total = own_part[j][z]
        for step in range(1, n_z):
            sum_z(j, step).wait_recv()
            total = total + z_recv[j][step].astype(F32)
        raw[:, spans[j]] = total
        back_send[j][...] = fold(total[CAP:])
        hand_back(j).start()

    def collect(j):
        hand_back(j).wait_recv()
        out[:, spans[j]] = jnp.concatenate(
            [raw[:CAP, spans[j]], unfold(back_recv[j][...])], axis=0
        ).astype(BF16)

    pair_up(0)
    for j in range(n_s):
        if j + 1 < n_s:
            pair_up(j + 1)
        finish(j)
        if j >= 1:
            collect(j - 1)
    collect(n_s - 1)

    for k in range(n_c):
        exchange(k).wait_send()
        for step in range(n_z):
            along_y(k, z_from[step]).wait_send()
        for step in range(1, n_z):
            along_z(k, step).wait_send()
    for j in range(n_s):
        for step in range(1, n_z):
            sum_z(j, step).wait_send()
        sum_y(j).wait_send()
        hand_back(j).wait_send()


def combine(coefs, tokens, expert_out, out):
    rows = expert_out[...]
    added = jnp.dot(
        coefs[...], jnp.concatenate([rows, rows, rows], axis=0), preferred_element_type=F32
    )
    out[...] = (tokens[...].astype(F32) + added).astype(BF16)


def fused(n_z, tokens, norm_gain, routes, router_logits, gate_proj, up_proj, down_proj):
    n_c, n_s = N_CHUNKS, len(SUM_WIDTHS)
    count, depth = tokens.shape
    width = depth // n_c
    units = gate_proj.shape[2]
    rows = 2 * CAP
    everyone = 2 * n_z * rows
    vmem, hbm = pl.BlockSpec(memory_space=pltpu.VMEM), pl.BlockSpec(memory_space=pl.ANY)
    dma = pltpu.SemaphoreType.DMA
    routes_t, logits_t = routes.T, router_logits.T
    expert_out, coefs = pl.pallas_call(
        functools.partial(experts, n_z, n_c, n_s),
        out_shape=[
            jax.ShapeDtypeStruct((rows, depth), BF16),
            jax.ShapeDtypeStruct((count, 3 * rows), BF16),
        ],
        in_specs=[hbm, vmem, vmem, vmem, hbm, hbm, hbm],
        out_specs=[vmem, vmem],
        scratch_shapes=[
            pltpu.VMEM((n_c, count, width), BF16),
            pltpu.VMEM((n_c, units, width), BF16),
            pltpu.VMEM((n_c, units, width), BF16),
            pltpu.VMEM((units, depth), BF16),
            pltpu.VMEM((rows, depth), F32),
            pltpu.VMEM((n_c, rows, width // 2), BF16),
            pltpu.VMEM((n_c, rows, width // 2), BF16),
            pltpu.VMEM((n_c, 2 * n_z, rows, width), BF16),
            pltpu.VMEM((everyone, units), F32),
            pltpu.VMEM((everyone, units), F32),
            pltpu.VMEM((everyone, units), BF16),
            tuple(pltpu.VMEM((n_z, rows, wide), F32) for wide in SUM_WIDTHS),
            tuple(pltpu.VMEM((n_z, rows, wide), BF16) for wide in SUM_WIDTHS),
            tuple(pltpu.VMEM((n_z, rows, wide), BF16) for wide in SUM_WIDTHS),
            tuple(pltpu.VMEM((n_z, rows, wide), BF16) for wide in SUM_WIDTHS),
            tuple(pltpu.VMEM((n_z, rows, wide), BF16) for wide in SUM_WIDTHS),
            tuple(pltpu.VMEM((rows, wide // 2), BF16) for wide in SUM_WIDTHS),
            tuple(pltpu.VMEM((rows, wide // 2), BF16) for wide in SUM_WIDTHS),
            dma((n_c,)),
            dma((2, n_c)),
            dma((n_s,)),
            dma((2, n_c)),
            dma((n_z, n_c)),
            dma((n_z, n_c)),
            dma((n_z, n_c)),
            dma((n_z, n_c)),
            dma((2, n_s)),
            dma((n_z, n_s)),
            dma((n_z, n_s)),
            dma((2, n_s)),
        ],
        compiler_params=pltpu.CompilerParams(
            collective_id=0, has_side_effects=True, vmem_limit_bytes=58 * 1024 * 1024
        ),
    )(
        tokens, norm_gain.reshape(1, depth), routes_t, logits_t,
        jnp.swapaxes(gate_proj, 1, 2), jnp.swapaxes(up_proj, 1, 2), down_proj,
    )
    steps = 2
    tile = depth // steps
    return pl.pallas_call(
        combine,
        grid=(steps,),
        out_shape=jax.ShapeDtypeStruct(tokens.shape, BF16),
        in_specs=[
            vmem,
            pl.BlockSpec((count, tile), lambda i: (0, i)),
            pl.BlockSpec((rows, tile), lambda i: (0, i)),
        ],
        out_specs=pl.BlockSpec((count, tile), lambda i: (0, i)),
    )(coefs, tokens, expert_out)


def solution(mesh):
    placed = (
        P(("groups", "wide", "narrow"), None),
        P(),
        P(("groups", "wide", "narrow"), None),
        P(("groups", "wide", "narrow"), None),
        P("narrow", None, "wide"),
        P("narrow", None, "wide"),
        P("narrow", "wide", None),
    )
    fits = mesh.shape["wide"] == 8 and mesh.shape["narrow"] == 2
    return jax.shard_map(
        functools.partial(fused, mesh.shape["wide"] // 2) if fits else shards,
        mesh=mesh,
        in_specs=placed,
        out_specs=P(("groups", "wide", "narrow"), None),
        check_vma=False,
    )
```

```python
import functools

import jax
import jax.numpy as jnp
from jax import lax
from jax.experimental import pallas as pl
from jax.experimental.pallas import tpu as pltpu
from jax.sharding import PartitionSpec as P

CAP = 8
N_CHUNKS = 4
SUM_WIDTHS = (1792, 1792, 1792, 1792)
MESH = pl.DeviceIdType.MESH
F32 = jnp.float32
BF16 = jnp.bfloat16


def normalize(tokens, norm_gain):
    wide_tok = tokens.astype(jnp.float32)
    scale = lax.rsqrt(jnp.mean(wide_tok * wide_tok, axis=1, keepdims=True) + 1e-05)
    return (wide_tok * scale * norm_gain).astype(jnp.bfloat16)


def slot_tables(routes, router_logits, flight, capacity):
    probs = jax.nn.softmax(router_logits, axis=1)
    expert_ids = lax.broadcasted_iota(jnp.int32, (1, 1, flight), 2)
    hits = routes[:, :, None] == expert_ids
    matched = jnp.sum(hits.astype(jnp.int32), axis=1)
    slot_rank = jnp.cumsum(matched, axis=0) - 1
    is_kept = (matched > 0) & (slot_rank < capacity)
    slot_ids = lax.broadcasted_iota(jnp.int32, (1, 1, capacity), 2)
    select = is_kept[:, :, None] & (slot_rank[:, :, None] == slot_ids)
    weights = jnp.sum(hits.astype(jnp.float32) * probs[:, :, None], axis=1) * is_kept.astype(
        jnp.float32
    )
    return (select, weights)


def expert_hidden(rows, gate_local, up_local):
    gate_act = jnp.dot(rows, gate_local, preferred_element_type=jnp.float32)
    up_act = jnp.dot(rows, up_local, preferred_element_type=jnp.float32)
    return (jax.nn.silu(gate_act) * up_act).astype(jnp.bfloat16)


def shards(tokens, norm_gain, routes, router_logits, gate_proj, up_proj, down_proj):
    flight = lax.axis_size("narrow")
    normed = normalize(tokens, norm_gain)
    select, weights = slot_tables(routes, router_logits, flight, CAP)
    buffer = jnp.einsum(
        "tfc,td->fcd", select.astype(jnp.bfloat16), normed, preferred_element_type=jnp.float32
    ).astype(jnp.bfloat16)
    gate_local = gate_proj[0]
    up_local = up_proj[0]
    owned = lax.all_to_all(buffer, "narrow", split_axis=0, concat_axis=1, tiled=True)
    hidden_all = expert_hidden(
        lax.all_gather(owned, "wide", axis=1, tiled=True)[0], gate_local, up_local
    )
    down_local = down_proj[0]
    summed = lax.psum_scatter(
        jnp.dot(hidden_all, down_local, preferred_element_type=jnp.float32).astype(jnp.bfloat16),
        "wide",
        scatter_dimension=0,
        tiled=True,
    )
    expert_out = summed.reshape(flight, CAP, summed.shape[1])
    returned = lax.all_to_all(expert_out, "narrow", split_axis=0, concat_axis=0, tiled=True)
    coefs = select.astype(jnp.float32) * weights[:, :, None]
    combined = jnp.einsum(
        "tfc,fcd->td", coefs, returned.astype(jnp.float32), precision=lax.Precision.HIGHEST
    )
    return (tokens.astype(jnp.float32) + combined).astype(jnp.bfloat16)


def picks(routes, narrow):
    count = routes.shape[1]
    row = lax.broadcasted_iota(jnp.int32, (2 * CAP, count), 0)
    own = row < CAP
    expert = jnp.where(own, narrow, 1 - narrow)
    slot = jnp.where(own, row, row - CAP)
    first = routes[0:1, :] == expert
    second = routes[1:2, :] == expert
    hit = first | second
    earlier = lax.broadcasted_iota(jnp.int32, (count, count), 0) < lax.broadcasted_iota(
        jnp.int32, (count, count), 1
    )
    rank = jnp.dot(
        jnp.where(hit, 1.0, 0.0).astype(BF16),
        jnp.where(earlier, 1.0, 0.0).astype(BF16),
        preferred_element_type=F32,
    )
    return first, second, hit & (rank == slot.astype(F32))


def fold(rows):
    half = rows.shape[1] // 2
    return jnp.concatenate([rows[:, :half], rows[:, half:]], axis=0).astype(BF16)


def unfold(packed):
    wide = packed.astype(F32)
    return jnp.concatenate([wide[:CAP], wide[CAP:]], axis=1)


def experts(
    n_z, n_c, n_s, tokens_hbm, gain, routes, logits, gate_hbm, up_hbm, down_hbm, out, coefs,
    tok, gate, up, down, raw, give, got, gathered, gate_acc, up_acc, hidden,
    own_part, y_send, y_recv, z_send, z_recv, back_send, back_recv,
    tok_sem, w_sem, d_sem, x_sem, gz_send, gz_recv, gy_send, gy_recv,
    ry_sem, rz_send, rz_recv, b_sem,
):
    wide, narrow = lax.axis_index("wide"), lax.axis_index("narrow")
    z, y = lax.div(wide, 2), lax.rem(wide, 2)
    width = tok.shape[2]
    rows = 2 * CAP
    y_peer = {"wide": 2 * z + 1 - y}
    sibling = {"narrow": 1 - narrow}
    z_at = [lax.rem(z + step, n_z) for step in range(n_z)]
    z_from = [lax.rem(z + n_z - step, n_z) for step in range(n_z)]

    def z_peer(step):
        return {"wide": 2 * z_at[step] + y}

    def remote(source, target, send, recv, device):
        return pltpu.make_async_remote_copy(
            src_ref=source, dst_ref=target, send_sem=send, recv_sem=recv,
            device_id=device, device_id_type=MESH,
        )

    def columns(k):
        return pl.ds(pl.multiple_of(k * width, 128), width)

    def token_copy(k):
        return pltpu.make_async_copy(tokens_hbm.at[:, columns(k)], tok.at[k], tok_sem.at[k])

    def weight_copies(k):
        return (
            pltpu.make_async_copy(gate_hbm.at[0, :, columns(k)], gate.at[k], w_sem.at[0, k]),
            pltpu.make_async_copy(up_hbm.at[0, :, columns(k)], up.at[k], w_sem.at[1, k]),
        )

    starts = [sum(SUM_WIDTHS[:j]) for j in range(n_s)]
    spans = [pl.ds(starts[j], SUM_WIDTHS[j]) for j in range(n_s)]

    def down_copy(j):
        return pltpu.make_async_copy(down_hbm.at[0, :, spans[j]], down.at[:, spans[j]], d_sem.at[j])

    def exchange(k):
        return remote(give.at[k], got.at[k], x_sem.at[0, k], x_sem.at[1, k], sibling)

    def along_z(k, step):
        return remote(
            gathered.at[k, z], gathered.at[k, z], gz_send.at[step, k], gz_recv.at[z, k], z_peer(step)
        )

    def from_z(k, step):
        at = z_from[step]
        return remote(
            gathered.at[k, at], gathered.at[k, at], gz_send.at[step, k], gz_recv.at[at, k], z_peer(step)
        )

    def along_y(k, at):
        return remote(
            gathered.at[k, at], gathered.at[k, n_z + at], gy_send.at[at, k], gy_recv.at[at, k], y_peer
        )

    def sum_y(j):
        return remote(
            y_send[j], y_recv[j], ry_sem.at[0, j], ry_sem.at[1, j],
            y_peer,
        )

    def sum_z(j, step):
        return remote(
            z_send[j].at[z_at[step]], z_recv[j].at[step], rz_send.at[step, j],
            rz_recv.at[step, j], z_peer(step),
        )

    def hand_back(j):
        return remote(
            back_send[j], back_recv[j], b_sem.at[0, j], b_sem.at[1, j],
            sibling,
        )

    for k in range(n_c):
        token_copy(k).start()
    barrier = pltpu.get_barrier_semaphore()
    for peer in [sibling, y_peer] + [z_peer(step) for step in range(1, n_z)]:
        pl.semaphore_signal(barrier, inc=1, device_id=peer, device_id_type=MESH)

    first, second, kept = picks(routes[...], narrow)
    chosen = jnp.where(kept, 1.0, 0.0).astype(BF16)
    squares = jnp.zeros((rows, 1), F32)
    for k in range(n_c):
        token_copy(k).wait()
        picked = jnp.dot(chosen, tok[k], preferred_element_type=F32)
        raw[:, k * width : (k + 1) * width] = picked
        squares = squares + jnp.sum(picked * picked, axis=1, keepdims=True)
    for k in range(n_c):
        for copy in weight_copies(k):
            copy.start()
    for j in range(n_s):
        down_copy(j).start()
    pl.semaphore_wait(barrier, n_z + 1)
    scale = lax.rsqrt(squares / (n_c * width) + 1e-05)
    for k in range(n_c):
        normed = raw[:, k * width : (k + 1) * width] * scale * gain[0:1, k * width : (k + 1) * width]
        raw[:, k * width : (k + 1) * width] = normed
        give[k] = fold(normed[CAP:])
        exchange(k).start()
    for k in range(n_c):
        exchange(k).wait_recv()
        gathered[k, z] = jnp.concatenate(
            [raw[:CAP, k * width : (k + 1) * width], unfold(got[k])], axis=0
        ).astype(BF16)
        along_y(k, z).start()
        for step in range(1, n_z):
            along_z(k, step).start()
    values = logits[...]
    powers = jnp.exp(values - jnp.max(values, axis=0, keepdims=True))
    probs = powers / jnp.sum(powers, axis=0, keepdims=True)
    weight = jnp.where(first, probs[0:1, :], 0.0) + jnp.where(second, probs[1:2, :], 0.0)
    rest = jnp.where(kept, weight, 0.0)
    pieces = []
    for _ in range(3):
        rounded = rest.astype(BF16).astype(F32)
        pieces.append(rounded)
        rest = rest - rounded
    coefs[...] = jnp.concatenate(pieces, axis=0).T.astype(BF16)
    gate_acc[...] = jnp.zeros_like(gate_acc)
    up_acc[...] = jnp.zeros_like(up_acc)

    def pass_on(k):
        for step in range(1, n_z):
            from_z(k, step).wait_recv()
            along_y(k, z_from[step]).start()

    pass_on(0)

    def take(k, carry):
        @pl.when(k + 1 < n_c)
        def _():
            pass_on(k + 1)

        for step in range(n_z):
            along_y(k, z_from[step]).wait_recv()
        for copy in weight_copies(k):
            copy.wait()
        block = gathered[k].reshape(2 * n_z * rows, width)
        gate_acc[...] += lax.dot_general(
            block, gate[k], (((1,), (1,)), ((), ())), preferred_element_type=F32
        )
        up_acc[...] += lax.dot_general(
            block, up[k], (((1,), (1,)), ((), ())), preferred_element_type=F32
        )
        return carry

    lax.fori_loop(0, n_c, take, 0)
    gated = gate_acc[...]
    hidden[...] = (gated / (1.0 + jnp.exp(-gated)) * up_acc[...]).astype(BF16)

    half = n_z * rows
    def part(j):
        down_copy(j).wait()
        product = jnp.dot(hidden[...], down[:, spans[j]], preferred_element_type=F32)
        y_send[j][...] = product[half:].astype(BF16).reshape(n_z, rows, SUM_WIDTHS[j])
        sum_y(j).start()
        own_part[j][...] = product[:half].reshape(n_z, rows, SUM_WIDTHS[j])

    def pair_up(j):
        sum_y(j).wait_recv()
        both = own_part[j][...] + y_recv[j][...].astype(F32)
        own_part[j][...] = both
        z_send[j][...] = both.astype(BF16)
        for step in range(1, n_z):
            sum_z(j, step).start()

    def finish(j):
        total = own_part[j][z]
        for step in range(1, n_z):
            sum_z(j, step).wait_recv()
            total = total + z_recv[j][step].astype(F32)
        raw[:, spans[j]] = total
        back_send[j][...] = fold(total[CAP:])
        hand_back(j).start()

    def collect(j):
        hand_back(j).wait_recv()
        out[:, spans[j]] = jnp.concatenate(
            [raw[:CAP, spans[j]], unfold(back_recv[j][...])], axis=0
        ).astype(BF16)

    part(0)
    part(1)
    for j in range(n_s):
        pair_up(j)
        if j + 2 < n_s:
            part(j + 2)
        if j >= 1:
            finish(j - 1)
        if j >= 2:
            collect(j - 2)
    finish(n_s - 1)
    collect(n_s - 2)
    collect(n_s - 1)

    for k in range(n_c):
        exchange(k).wait_send()
        for step in range(n_z):
            along_y(k, z_from[step]).wait_send()
        for step in range(1, n_z):
            along_z(k, step).wait_send()
    for j in range(n_s):
        for step in range(1, n_z):
            sum_z(j, step).wait_send()
        sum_y(j).wait_send()
        hand_back(j).wait_send()


def combine(coefs, tokens, expert_out, out):
    rows = expert_out[...]
    added = jnp.dot(
        coefs[...], jnp.concatenate([rows, rows, rows], axis=0), preferred_element_type=F32
    )
    out[...] = (tokens[...].astype(F32) + added).astype(BF16)


def fused(n_z, tokens, norm_gain, routes, router_logits, gate_proj, up_proj, down_proj):
    n_c, n_s = N_CHUNKS, len(SUM_WIDTHS)
    count, depth = tokens.shape
    width = depth // n_c
    units = gate_proj.shape[2]
    rows = 2 * CAP
    everyone = 2 * n_z * rows
    vmem, hbm = pl.BlockSpec(memory_space=pltpu.VMEM), pl.BlockSpec(memory_space=pl.ANY)
    dma = pltpu.SemaphoreType.DMA
    routes_t, logits_t = routes.T, router_logits.T
    expert_out, coefs = pl.pallas_call(
        functools.partial(experts, n_z, n_c, n_s),
        out_shape=[
            jax.ShapeDtypeStruct((rows, depth), BF16),
            jax.ShapeDtypeStruct((count, 3 * rows), BF16),
        ],
        in_specs=[hbm, vmem, vmem, vmem, hbm, hbm, hbm],
        out_specs=[vmem, vmem],
        scratch_shapes=[
            pltpu.VMEM((n_c, count, width), BF16),
            pltpu.VMEM((n_c, units, width), BF16),
            pltpu.VMEM((n_c, units, width), BF16),
            pltpu.VMEM((units, depth), BF16),
            pltpu.VMEM((rows, depth), F32),
            pltpu.VMEM((n_c, rows, width // 2), BF16),
            pltpu.VMEM((n_c, rows, width // 2), BF16),
            pltpu.VMEM((n_c, 2 * n_z, rows, width), BF16),
            pltpu.VMEM((everyone, units), F32),
            pltpu.VMEM((everyone, units), F32),
            pltpu.VMEM((everyone, units), BF16),
            tuple(pltpu.VMEM((n_z, rows, wide), F32) for wide in SUM_WIDTHS),
            tuple(pltpu.VMEM((n_z, rows, wide), BF16) for wide in SUM_WIDTHS),
            tuple(pltpu.VMEM((n_z, rows, wide), BF16) for wide in SUM_WIDTHS),
            tuple(pltpu.VMEM((n_z, rows, wide), BF16) for wide in SUM_WIDTHS),
            tuple(pltpu.VMEM((n_z, rows, wide), BF16) for wide in SUM_WIDTHS),
            tuple(pltpu.VMEM((rows, wide // 2), BF16) for wide in SUM_WIDTHS),
            tuple(pltpu.VMEM((rows, wide // 2), BF16) for wide in SUM_WIDTHS),
            dma((n_c,)),
            dma((2, n_c)),
            dma((n_s,)),
            dma((2, n_c)),
            dma((n_z, n_c)),
            dma((n_z, n_c)),
            dma((n_z, n_c)),
            dma((n_z, n_c)),
            dma((2, n_s)),
            dma((n_z, n_s)),
            dma((n_z, n_s)),
            dma((2, n_s)),
        ],
        compiler_params=pltpu.CompilerParams(
            collective_id=0, has_side_effects=True, vmem_limit_bytes=58 * 1024 * 1024
        ),
    )(
        tokens, norm_gain.reshape(1, depth), routes_t, logits_t,
        jnp.swapaxes(gate_proj, 1, 2), jnp.swapaxes(up_proj, 1, 2), down_proj,
    )
    steps = 2
    tile = depth // steps
    return pl.pallas_call(
        combine,
        grid=(steps,),
        out_shape=jax.ShapeDtypeStruct(tokens.shape, BF16),
        in_specs=[
            vmem,
            pl.BlockSpec((count, tile), lambda i: (0, i)),
            pl.BlockSpec((rows, tile), lambda i: (0, i)),
        ],
        out_specs=pl.BlockSpec((count, tile), lambda i: (0, i)),
    )(coefs, tokens, expert_out)


def solution(mesh):
    placed = (
        P(("groups", "wide", "narrow"), None),
        P(),
        P(("groups", "wide", "narrow"), None),
        P(("groups", "wide", "narrow"), None),
        P("narrow", None, "wide"),
        P("narrow", None, "wide"),
        P("narrow", "wide", None),
    )
    fits = mesh.shape["wide"] == 8 and mesh.shape["narrow"] == 2
    return jax.shard_map(
        functools.partial(fused, mesh.shape["wide"] // 2) if fits else shards,
        mesh=mesh,
        in_specs=placed,
        out_specs=P(("groups", "wide", "narrow"), None),
        check_vma=False,
    )
```
